512 devices in a mesh: dp: 16 (over z_lo, core), fsdp: 32 (over y, z_hi, x).
Axes of the slice: x: 4, y: 4, z: 16 (z_hi: 2, z_lo: 8; z = z_hi * 8 + z_lo), core: 2. Of those that a mesh axis runs over, the one named last changes fastest.
Arguments:
- queries: bfloat16 [2048, 4096], P('dp', 'fsdp'), as said below
- passages: bfloat16 [2048, 4096], P('dp', 'fsdp'), as said below
- positive: int32 [2048], P('dp'), may hold values from 0 to 2047, each once
- hidden_states: bfloat16 [262144, 4096], P(('dp', 'fsdp')), may hold values from -6 to 6
- lengths: int32 [2048], P(('dp', 'fsdp')), may hold values from 1 to 128, as said below
- w_down: bfloat16 [4096, 128], P('fsdp'), may hold values from -0.09375 to 0.09375
- w_up: bfloat16 [128, 4096], P(None, 'fsdp'), may hold values from -0.5 to 0.5
Outputs:
- grad_queries: bfloat16 [2048, 4096], P('dp', 'fsdp')
- grad_passages: bfloat16 [2048, 4096], P('dp', 'fsdp')
- sub_embed: bfloat16 [2048, 4096], P(('dp', 'fsdp'))
- grad_down: float32 [4096, 128], P('fsdp')
- grad_up: float32 [128, 4096], P(None, 'fsdp')
The draws below stay inside these ranges and needn't reach their ends.
Inputs may be any that keep to these rules, and one draw needn't show every extreme that they name: `queries`: entries of the cached query embeddings lie within -0.2 to 0.2. `passages`: entries of the cached page embeddings lie within -0.25 to 0.25. `lengths`: in every draw some page has length 128 and some page has length 1.
All inputs are finite; a program needn't handle non-finite values.
Results may differ from the reference program's by a relative error of at most 0.022.
Values may be sent and summed in bfloat16 or wider, within the bound.
No kernel may reach another device: no remote copies, remote signals or barrier semaphores. Data moves between devices by JAX's collectives and lax.ppermute only.
A program may use at most 64 MiB of HBM per device.

```python
import jax
import jax.numpy as jnp
from jax import lax

D = 4096
R = 128
PAIRS_DP = 128
SEQ_DEV = 4
LEN = 128
PAIRS = 2048
SEQS = 2048
N_DP = 16
N_FSDP = 32


def draw_queries(key, part):
    key = jax.random.fold_in(key, 1)
    values = jnp.clip(0.05 * jax.random.normal(key, (PAIRS, D), jnp.float32), -0.2, 0.2)
    return values.astype(jnp.bfloat16)


def draw_passages(key, part):
    key = jax.random.fold_in(key, 2)
    values = jnp.clip(0.05 * jax.random.normal(key, (PAIRS, D), jnp.float32), -0.2, 0.2)
    return values.astype(jnp.bfloat16)


def draw_lengths(key, part):
    key = jax.random.fold_in(key, 3)
    values = jax.random.randint(key, (SEQS,), 1, LEN + 1, dtype=jnp.int32)
    values = values.at[0].set(LEN)
    return values.at[1].set(1)


def block_scale(key, dims, cuts, smallest, top_value):
    def one(dim, parts):
        heights = jax.random.uniform(jax.random.fold_in(jax.random.fold_in(key, 6), dim), (parts,), jnp.float32, smallest / len(cuts), top_value / len(cuts))
        return jnp.repeat(jnp.exp(heights), dims[dim] // parts).reshape((-1,) + (1,) * (len(dims) - dim - 1))

    gain = one(*cuts[0])
    for cut in cuts[1:]:
        gain = gain * one(*cut)
    return gain


def bell_draw(own_key, extent, spread, limit, pieces=(), kind=jnp.bfloat16):
    values = jax.random.normal(own_key, extent, jnp.float32) * spread
    if len(pieces) > 0:
        values = block_scale(own_key, extent, pieces, -0.22, 0.18) * values
    return jnp.clip(values, min=-limit, max=limit).astype(kind)


def setup_inputs(seed: int = 0) -> dict:
    seeds = jax.random.split(jax.random.key(seed), 8)
    return {
        "queries": draw_queries(jax.random.fold_in(seeds[7], 71), 0),
        "passages": draw_passages(jax.random.fold_in(seeds[7], 71), 0),
        "positive": jax.random.permutation(seeds[2], PAIRS).astype(jnp.int32),
        "hidden_states": bell_draw(seeds[3], (SEQS * LEN, D), 1.0, 6.0, ((0, 512),)),
        "lengths": draw_lengths(jax.random.fold_in(seeds[7], 71), 0),
        "w_down": bell_draw(seeds[5], (D, R), D ** -0.5, 0.09375, ((0, 32),)),
        "w_up": bell_draw(seeds[6], (R, D), R ** -0.5, 0.5, ((1, 32),)),
    }


inv_temp = 20.0
eps = 1e-06

def adapter_terms(block_x, block_len, block_cot, w_down, w_up):
    xf = block_x.astype(jnp.float32)
    mean_sq = lax.optimization_barrier(jnp.mean(xf * xf, axis=-1, keepdims=True))
    normed = (xf * lax.rsqrt(mean_sq + eps)).astype(jnp.bfloat16)
    pre = jnp.dot(normed, w_down, preferred_element_type=jnp.float32)
    act = jax.nn.silu(pre).astype(jnp.bfloat16)
    out = xf + jnp.dot(act, w_up, preferred_element_type=jnp.float32)
    pages = block_len.shape[0]
    page_len = block_x.shape[0] // pages
    places = jnp.arange(page_len, dtype=jnp.int32)
    valid = (places[None, :] < block_len[:, None]).astype(jnp.float32)
    weight = valid / block_len.astype(jnp.float32)[:, None]
    out3 = out.reshape(pages, page_len, out.shape[1])
    embed = lax.optimization_barrier(jnp.sum(weight[:, :, None] * out3, axis=1)).astype(jnp.bfloat16)
    act3 = act.astype(jnp.float32).reshape(pages, page_len, act.shape[1])
    pooled = lax.optimization_barrier(jnp.sum(weight[:, :, None] * act3, axis=1)).astype(jnp.bfloat16)
    dout = (weight[:, :, None] * block_cot.astype(jnp.float32)[:, None, :]).reshape(block_x.shape[0], -1).astype(jnp.bfloat16)
    up_part = lax.dot_general(pooled, block_cot, (((0,), (0,)), ((), ())), preferred_element_type=jnp.float32)
    dact = lax.dot_general(dout, w_up, (((1,), (1,)), ((), ())), preferred_element_type=jnp.float32)
    sig = jax.nn.sigmoid(pre)
    dpre = (dact * sig * (1.0 + pre * (1.0 - sig))).astype(jnp.bfloat16)
    down_part = jnp.dot(normed.T, dpre, preferred_element_type=jnp.float32)
    return (embed, down_part, up_part)

def reference(queries, passages, positive, hidden_states, lengths, w_down, w_up):
    scores = inv_temp * lax.dot_general(queries, passages, (((1,), (1,)), ((), ())), preferred_element_type=jnp.float32)
    probs = jax.nn.softmax(scores, axis=-1)
    columns = jnp.arange(PAIRS, dtype=jnp.int32)
    onehot = (positive[:, None] == columns[None, :]).astype(jnp.float32)
    coeff = (probs - onehot).astype(jnp.bfloat16)
    grad_queries = (inv_temp * jnp.dot(coeff, passages, preferred_element_type=jnp.float32)).astype(jnp.bfloat16)
    grad_passages = (inv_temp * lax.dot_general(coeff, queries, (((0,), (0,)), ((), ())), preferred_element_type=jnp.float32)).astype(jnp.bfloat16)
    blocks = N_DP * N_FSDP
    cot = grad_passages.reshape(N_DP, PAIRS_DP, D)[:, :SEQ_DEV * N_FSDP].reshape(blocks, SEQ_DEV, D)
    xs = (hidden_states.reshape(blocks, SEQ_DEV * LEN, D), lengths.reshape(blocks, SEQ_DEV), cot)

    def step(carry, item):
        embed, down_part, up_part = adapter_terms(item[0], item[1], item[2], w_down, w_up)
        down_sum = carry[0] + down_part.astype(jnp.bfloat16).astype(jnp.float32)
        up_sum = carry[1] + up_part.astype(jnp.bfloat16).astype(jnp.float32)
        return ((down_sum, up_sum), embed)
    start = (jnp.zeros((D, R), jnp.float32), jnp.zeros((R, D), jnp.float32))
    (grad_down, grad_up), embeds = lax.scan(step, start, xs)
    sub_embed = embeds.reshape(SEQS, D)
    return (grad_queries, grad_passages, sub_embed, grad_down, grad_up)
```

```python
import jax
import jax.numpy as jnp
import numpy as np
from jax import lax
from jax.sharding import Mesh, PartitionSpec as P

inv_temp = 20.0
eps = 1e-06
bf16 = jnp.bfloat16
f32 = jnp.float32


def exchange(x, axes):
    return lax.all_to_all(x, axes, split_axis=0, concat_axis=0, tiled=False)


def spread(x, count):
    return jnp.broadcast_to(x[None], (count,) + x.shape)


def swap(x, axis):
    return lax.ppermute(x, axis, [(0, 1), (1, 0)])


def in_order(first, mine, other):
    return jnp.where(first, jnp.stack([mine, other]), jnp.stack([other, mine]))


def local(queries, passages, positive, hidden, lengths, w_down, w_up):
    zl_n, y_n, x_n = lax.axis_size("zl"), lax.axis_size("y"), lax.axis_size("x")
    c, y, h, x = (lax.axis_index(a) for a in ("c", "y", "h", "x"))
    plane = y_n * x_n
    rows, width = queries.shape
    pages, rank = lengths.shape[0], w_down.shape[1]
    tokens = hidden.shape[0]
    half = plane * pages

    pack = jnp.concatenate([queries, w_up, w_down], axis=0)
    both = in_order(h == 0, pack, swap(pack, "h"))
    q_mine = both[:, :rows]
    up2 = both[:, rows : rows + rank]
    down2 = both[:, rows + rank :]
    q_both = in_order(c == 0, q_mine, swap(q_mine, "c"))
    q_all = q_both.transpose(0, 2, 1, 3).reshape(2 * rows, 2 * width)

    p_sub = passages.reshape(y_n, 2, x_n * pages, width).transpose(1, 0, 2, 3)
    p_sub = p_sub.reshape(2, half, width)
    p_got = exchange(spread(p_sub, zl_n).reshape(zl_n * 2, half, width), ("zl", "h"))
    p_all = p_got.reshape(zl_n, 2, half, width).transpose(0, 2, 1, 3)
    p_all = p_all.reshape(zl_n * half, 2 * width)
    cols = zl_n * half

    part = lax.dot_general(q_all, p_all, (((1,), (1,)), ((), ())), preferred_element_type=f32)
    q_c = jnp.where(c == 0, q_all[:, :width], q_all[:, width:])
    up_c = jnp.where(c == 0, up2[0], up2[1])
    qw_part = lax.dot_general(q_c, up_c, (((1,), (1,)), ((), ())), preferred_element_type=f32)
    own = 2 * rows // (2 * plane)
    sent = jnp.concatenate([part, qw_part], axis=1).reshape(2 * plane, own, cols + rank)
    got = jnp.sum(exchange(sent, ("c", "y", "x")).reshape(2, plane, own, cols + rank), axis=1)
    scores = inv_temp * got[:, :, :cols]
    qw = got[0, :, cols:] + got[1, :, cols:]
    top = jnp.max(scores, axis=(0, 2))
    e = jnp.exp(scores - top[None, :, None])
    total = jnp.sum(e, axis=(0, 2))
    lane = lax.broadcasted_iota(jnp.int32, (own, 128), 1)
    stats = swap(jnp.where(lane < 64, top[:, None], total[:, None]), "h")
    top_o, total_o = stats[:, 0], stats[:, 64]
    top_a = jnp.maximum(top, top_o)
    scale = jnp.exp(top - top_a)
    z = total * scale + total_o * jnp.exp(top_o - top_a)
    probs = e * (scale / z)[None, :, None]
    k = np.arange(cols)
    base = k // half * (4 * half) + k % half // (x_n * pages) * (2 * x_n * pages) + k % (x_n * pages)
    base = np.stack([base, base + 2 * half]).astype(np.int32)
    target = lax.dynamic_slice(positive, ((y * x_n + x) * own,), (own,)) - h * (x_n * pages)
    onehot = (target[None, :, None] == base[:, None, :]).astype(f32)
    coeff_own = (probs - onehot).astype(bf16)
    qw_b = jnp.broadcast_to(qw.astype(bf16)[None], (2, own, rank))
    sent = jnp.concatenate([coeff_own, qw_b], axis=2)
    sent = jnp.broadcast_to(sent[:, None], (2, plane, own, cols + rank))
    got = exchange(sent.reshape(2 * plane, own, cols + rank), ("c", "y", "x"))
    got = got.reshape(2 * rows, cols + rank)
    coeff, qw_all = got[:, :cols], got[:, cols:]

    c_mine = coeff.reshape(2 * rows, zl_n, plane, pages)
    c_mine = lax.dynamic_slice_in_dim(c_mine, y * x_n + x, 1, axis=2)[:, :, 0]
    dact_part = lax.dot_general(
        c_mine.reshape(2 * rows, zl_n * pages), qw_all, (((0,), (0,)), ((), ())), preferred_element_type=f32
    )
    dact = inv_temp * jnp.sum(exchange(dact_part.reshape(zl_n, pages, rank), ("zl",)), axis=0)

    wd = exchange(spread(down2, plane), ("y", "x"))
    wd = wd.reshape(y_n, x_n, 2, width, rank).transpose(0, 2, 1, 3, 4).reshape(-1, rank)
    xf = hidden.astype(f32)
    rs = lax.rsqrt(jnp.mean(xf * xf, axis=-1, keepdims=True) + eps)
    normed = (xf * rs).astype(bf16)
    pre = jnp.dot(normed, wd, preferred_element_type=f32)
    sig = jax.nn.sigmoid(pre)
    act = (pre * sig).astype(bf16)
    span = tokens // pages
    place = jnp.arange(tokens, dtype=jnp.int32)
    page_of, at = place // span, place % span
    mask = (page_of[None, :] == jnp.arange(pages)[:, None]) & (at[None, :] < lengths[:, None])
    mask = mask.astype(bf16)
    inv_len = 1.0 / lengths.astype(f32)
    x_mean = jnp.dot(mask, hidden, preferred_element_type=f32) * inv_len[:, None]
    pooled = (jnp.dot(mask, act, preferred_element_type=f32) * inv_len[:, None]).astype(bf16)
    weight = (at.reshape(pages, span) < lengths[:, None]).astype(f32) * inv_len[:, None]
    g = (sig * (1.0 + pre * (1.0 - sig)) * rs).reshape(pages, span, rank) * weight[:, :, None]

    pooled_xy = exchange(spread(pooled, plane), ("y", "x")).reshape(half, rank)
    pooled_all = exchange(spread(pooled_xy, zl_n), ("zl",)).reshape(cols, rank)
    lift = jnp.einsum("pr,hrf->phf", pooled_xy, up2, preferred_element_type=f32)
    lift = exchange(lift.reshape(plane, pages, 2 * width), ("y", "x"))
    lift = lift.reshape(y_n, x_n, pages, 2, width).transpose(2, 0, 3, 1, 4).reshape(pages, -1)
    sub_embed = (x_mean + lift).astype(bf16)

    gp = lax.dot_general(coeff, q_all, (((0,), (0,)), ((), ())), preferred_element_type=f32)
    gp = gp.astype(bf16).reshape(zl_n, half, 2, width).transpose(0, 2, 1, 3)
    gp = exchange(gp.reshape(zl_n * 2, half, width), ("zl", "h")).astype(f32)
    gp = inv_temp * jnp.sum(gp.reshape(zl_n, 2, half, width), axis=0)
    grad_passages = gp.reshape(2, y_n, x_n * pages, width).transpose(1, 0, 2, 3)
    grad_passages = grad_passages.reshape(-1, width).astype(bf16)
    gq = jnp.dot(coeff, p_all, preferred_element_type=f32)
    gq = gq.reshape(2, rows, 2, width).transpose(0, 2, 1, 3).astype(bf16)
    gq = exchange(gq.reshape(4, rows, width), ("c", "h")).astype(f32)
    grad_queries = (inv_temp * jnp.sum(gq, axis=0)).astype(bf16)

    u = (inv_temp * jnp.dot(coeff, pooled_all, preferred_element_type=f32)).astype(bf16)
    up_part = lax.dot_general(u, q_all, (((0,), (0,)), ((), ())), preferred_element_type=f32)
    up_part = up_part.astype(bf16).reshape(zl_n, rank // zl_n, 2, width).transpose(0, 2, 1, 3)
    dpre = (g * dact[:, None, :]).astype(bf16).reshape(tokens, rank)
    down = lax.dot_general(dpre, hidden, (((0,), (0,)), ((), ())), preferred_element_type=f32)
    down = down.astype(bf16).reshape(2, rank // 2, y_n, 2, x_n, width).transpose(0, 2, 4, 3, 1, 5)
    down = exchange(down.reshape(2 * plane, 2, rank // 2, width), ("c", "y", "x")).astype(f32)
    down = jnp.sum(down, axis=0).astype(bf16)
    down = down.reshape(2, zl_n, rank // 2 // zl_n, width).transpose(1, 0, 2, 3)
    sent = jnp.concatenate([down, up_part], axis=2)
    step = sent.shape[2]
    got = exchange(sent.reshape(zl_n * 2, step, width), ("zl", "h")).astype(f32)
    got = exchange(spread(jnp.sum(got, axis=0), zl_n * 2), ("zl", "c"))
    got = got.reshape(zl_n, 2, step, width)
    n = rank // 2 // zl_n
    grad_down = got[:, :, :n].transpose(1, 0, 2, 3).reshape(rank, width).T
    grad_up = jnp.sum(got[:, :, n:], axis=1).reshape(rank, width)
    return (grad_queries, grad_passages, sub_embed, grad_down, grad_up)


def solution(mesh):
    dp, fsdp = ("zl", "c"), ("y", "h", "x")
    shape = (mesh.shape["dp"] // 2, 2, 4, 2, mesh.shape["fsdp"] // 8)
    inner = Mesh(mesh.devices.reshape(shape), dp + fsdp)
    both = dp + fsdp
    return jax.shard_map(
        local,
        mesh=inner,
        in_specs=(P(dp, fsdp), P(dp, fsdp), P(dp), P(both, None), P(both), P(fsdp, None), P(None, fsdp)),
        out_specs=(P(dp, fsdp), P(dp, fsdp), P(both, None), P(fsdp, None), P(None, fsdp)),
        check_vma=False,
    )
```

```python
import jax
import jax.numpy as jnp
import numpy as np
from jax import lax
from jax.sharding import Mesh, PartitionSpec as P

inv_temp = 20.0
eps = 1e-06
bf16 = jnp.bfloat16
f32 = jnp.float32


def exchange(x, axes):
    return lax.all_to_all(x, axes, split_axis=0, concat_axis=0, tiled=False)


def spread(x, count):
    return jnp.broadcast_to(x[None], (count,) + x.shape)


def swap(x, axis):
    return lax.ppermute(x, axis, [(0, 1), (1, 0)])


def in_order(first, mine, other):
    return jnp.where(first, jnp.stack([mine, other]), jnp.stack([other, mine]))


def split2(v):
    high = v.astype(bf16)
    return high, (v - high.astype(f32)).astype(bf16)


def local(queries, passages, positive, hidden, lengths, w_down, w_up):
    zl_n, y_n, x_n = lax.axis_size("zl"), lax.axis_size("y"), lax.axis_size("x")
    c, y, h, x = (lax.axis_index(a) for a in ("c", "y", "h", "x"))
    plane = y_n * x_n
    rows, width = queries.shape
    pages, rank = lengths.shape[0], w_down.shape[1]
    tokens = hidden.shape[0]
    half = plane * pages
    cols = zl_n * half
    own = rows // plane

    part = [lax.dynamic_slice_in_dim(w, c * (w.shape[0] // 2), w.shape[0] // 2) for w in (w_down, w_up)]
    pack = jnp.concatenate([queries] + part, axis=0)
    both = in_order(h == 0, pack, swap(pack, "h"))
    q_mine, w_both = both[:, :rows], both[:, rows:]
    q_both = in_order(c == 0, q_mine, swap(q_mine, "c"))
    q_all = q_both.transpose(0, 2, 1, 3).reshape(2 * rows, 2 * width)

    p_sub = passages.reshape(y_n, 2, x_n * pages, width).transpose(1, 0, 2, 3)
    p_sub = p_sub.reshape(2, half, width)
    p_got = exchange(spread(p_sub, zl_n).reshape(zl_n * 2, half, width), ("zl", "h"))
    p_all = p_got.reshape(zl_n, 2, half, width).transpose(0, 2, 1, 3)
    p_all = p_all.reshape(cols, 2 * width)

    part = lax.dot_general(q_all, p_all, (((1,), (1,)), ((), ())), preferred_element_type=f32)
    q_own = jnp.where(c == 0, jnp.stack([queries, q_both[1, h]]), jnp.stack([q_both[0, h], queries]))
    q_own = q_own.reshape(2 * rows, width)
    side = lax.broadcasted_iota(jnp.int32, (1, width), 1) // (width // 2) == c
    q_side = jnp.where(side, q_own, jnp.zeros_like(q_own))
    qw_part = lax.dot_general(q_side, w_up, (((1,), (1,)), ((), ())), preferred_element_type=f32)
    sent = jnp.concatenate([part, qw_part], axis=1).reshape(2 * plane, own, cols + rank)
    got = exchange(sent, ("c", "y", "x"))
    got, w_both = lax.optimization_barrier((got, w_both))
    got = jnp.sum(got.reshape(2, plane, own, cols + rank), axis=1)
    scores = inv_temp * got[:, :, :cols]
    qw = got[0, :, cols:] + got[1, :, cols:]
    top = jnp.max(scores, axis=(0, 2))
    e = jnp.exp(scores - top[None, :, None])
    total = jnp.sum(e, axis=(0, 2))
    lane = lax.broadcasted_iota(jnp.int32, (own, rank), 1)
    stats = jnp.where(lane < rank // 2, top[:, None], total[:, None])
    stats = swap(jnp.concatenate([stats, qw], axis=0), "h")
    w_half = exchange(spread(w_both, plane), ("y", "x"))
    top_o, total_o = stats[:own, 0], stats[:own, rank // 2]
    qw = qw + stats[own:]
    top_a = jnp.maximum(top, top_o)
    scale = jnp.exp(top - top_a)
    z = total * scale + total_o * jnp.exp(top_o - top_a)
    probs = e * (scale / z)[None, :, None]
    k = np.arange(cols)
    base = k // half * (4 * half) + k % half // (x_n * pages) * (2 * x_n * pages) + k % (x_n * pages)
    base = np.stack([base, base + 2 * half]).astype(np.int32)
    target = lax.dynamic_slice(positive, ((y * x_n + x) * own,), (own,)) - h * (x_n * pages)
    onehot = (target[None, :, None] == base[:, None, :]).astype(f32)
    coeff_own = (probs - onehot).astype(bf16)

    sent = jnp.broadcast_to(qw.astype(bf16)[None], (2, own, rank))
    sent = jnp.concatenate([coeff_own, sent], axis=2)
    step = cols + rank
    sent = jnp.broadcast_to(sent[:, None], (2, plane, own, step))
    sent, w_half = lax.optimization_barrier((sent, w_half))
    got = exchange(sent.reshape(2 * plane, own, step), ("c", "y", "x"))

    w_all = in_order(c == 0, w_half, swap(w_half, "c")).reshape(2, y_n, x_n, 2, -1, rank)
    wd = w_all[:, :, :, :, : width // 2].transpose(1, 3, 2, 0, 4, 5).reshape(-1, rank)
    wu = w_all[:, :, :, :, width // 2 :].transpose(0, 4, 1, 3, 2, 5).reshape(rank, -1)
    xf = hidden.astype(f32)
    rs = lax.rsqrt(jnp.mean(xf * xf, axis=-1, keepdims=True) + eps)
    normed = (xf * rs).astype(bf16)
    pre = jnp.dot(normed, wd, preferred_element_type=f32)
    sig = jax.nn.sigmoid(pre)
    act = (pre * sig).astype(bf16)
    span = tokens // pages
    place = jnp.arange(tokens, dtype=jnp.int32)
    page_of, at = place // span, place % span
    mask = (page_of[None, :] == jnp.arange(pages)[:, None]) & (at[None, :] < lengths[:, None])
    mask = mask.astype(bf16)
    inv_len = 1.0 / lengths.astype(f32)
    x_mean = jnp.dot(mask, hidden, preferred_element_type=f32) * inv_len[:, None]
    pooled = (jnp.dot(mask, act, preferred_element_type=f32) * inv_len[:, None]).astype(bf16)
    weight = (at.reshape(pages, span) < lengths[:, None]).astype(f32) * inv_len[:, None]
    g = (sig * (1.0 + pre * (1.0 - sig)) * rs).reshape(pages, span, rank) * weight[:, :, None]

    got, pooled, g = lax.optimization_barrier((got, pooled, g))
    got = got.reshape(2 * rows, step)
    coeff, qw_all = got[:, :cols], got[:, cols:]

    c_mine = coeff.reshape(2 * rows, zl_n, plane, pages)
    c_mine = lax.dynamic_slice_in_dim(c_mine, y * x_n + x, 1, axis=2)[:, :, 0]
    dact_part = lax.dot_general(
        c_mine.reshape(2 * rows, zl_n * pages), qw_all, (((0,), (0,)), ((), ())), preferred_element_type=f32
    )
    high, low = split2(dact_part.reshape(zl_n, pages, rank))
    gq = jnp.dot(coeff, p_all, preferred_element_type=f32).reshape(2, rows, 2 * width)
    got = exchange(jnp.concatenate([high, low, spread(pooled, zl_n)], axis=1), ("zl",))
    got, x_mean = lax.optimization_barrier((got, x_mean))
    dact = inv_temp * jnp.sum(got[:, : 2 * pages].astype(f32).reshape(zl_n, 2, pages, rank), axis=(0, 1))
    pooled_zl = got[:, 2 * pages :].reshape(zl_n * pages, rank)

    dpre = (g * dact[:, None, :]).astype(bf16).reshape(tokens, rank)
    first, second = dpre[:, : rank // 2], dpre[:, rank // 2 :]
    turn = (((0,), (0,)), ((), ()))
    theirs = lax.dot_general(jnp.where(c == 0, second, first), hidden, turn, preferred_element_type=f32)
    theirs = swap(theirs.astype(bf16), "c")
    mine = lax.dot_general(jnp.where(c == 0, first, second), hidden, turn, preferred_element_type=f32)
    down = (mine + theirs.astype(f32)).astype(bf16)
    down = down.reshape(rank // 2, y_n, 2, x_n, width).transpose(1, 3, 2, 0, 4).reshape(plane, rank, width)
    sent = jnp.concatenate([down, spread(pooled_zl, plane)], axis=1)
    sent, gq = lax.optimization_barrier((sent, gq))
    got = exchange(sent, ("y", "x"))
    gq = jnp.where(c == 0, gq[0], gq[1]) + swap(jnp.where(c == 0, gq[1], gq[0]), "c")
    pooled_all = got[:, rank:].reshape(plane, zl_n, pages, rank).transpose(1, 0, 2, 3).reshape(cols, rank)
    down = jnp.sum(got[:, :rank].astype(f32), axis=0).astype(bf16)
    down = down.reshape(2, zl_n, rank // 2 // zl_n, width).transpose(1, 0, 2, 3)

    sub_embed = (x_mean + jnp.dot(pooled, wu, preferred_element_type=f32)).astype(bf16)

    gp = lax.dot_general(coeff, q_all, (((0,), (0,)), ((), ())), preferred_element_type=f32)
    gp = gp.astype(bf16).reshape(zl_n, half, 2, width).transpose(0, 2, 1, 3)
    u = (inv_temp * jnp.dot(coeff, pooled_all, preferred_element_type=f32)).astype(bf16)
    up_part = lax.dot_general(u, q_all, (((0,), (0,)), ((), ())), preferred_element_type=f32)
    up_part = up_part.astype(bf16).reshape(zl_n, rank // zl_n, 2, width).transpose(0, 2, 1, 3)
    sent = jnp.concatenate([down, up_part, gp], axis=2)
    sent, gq = lax.optimization_barrier((sent, gq))
    got = exchange(sent.reshape(zl_n * 2, -1, width), ("zl", "h"))
    gq_0, gq_1 = gq[:, :width], gq[:, width:]
    gq = jnp.where(h == 0, gq_0, gq_1) + swap(jnp.where(h == 0, gq_1, gq_0), "h")
    grad_queries = (inv_temp * gq).astype(bf16)
    got, grad_queries = lax.optimization_barrier((got, grad_queries))
    got = got.astype(f32)
    n = rank // 2 // zl_n
    step = n + rank // zl_n
    weights = jnp.sum(got[:, :step], axis=0)
    gp = jnp.sum(got[:, step:].reshape(zl_n, 2, half, width), axis=0) * inv_temp
    grad_passages = gp.reshape(2, y_n, x_n * pages, width).transpose(1, 0, 2, 3)
    grad_passages = grad_passages.reshape(-1, width).astype(bf16)
    got = exchange(spread(weights, zl_n * 2), ("zl", "c")).reshape(zl_n, 2, step, width)
    grad_down = got[:, :, :n].transpose(1, 0, 2, 3).reshape(rank, width).T
    grad_up = jnp.sum(got[:, :, n:], axis=1).reshape(rank, width)
    return (grad_queries, grad_passages, sub_embed, grad_down, grad_up)


def solution(mesh):
    dp, fsdp = ("zl", "c"), ("y", "h", "x")
    shape = (mesh.shape["dp"] // 2, 2, 4, 2, mesh.shape["fsdp"] // 8)
    inner = Mesh(mesh.devices.reshape(shape), dp + fsdp)
    both = dp + fsdp
    return jax.shard_map(
        local,
        mesh=inner,
        in_specs=(P(dp, fsdp), P(dp, fsdp), P(dp), P(both, None), P(both), P(fsdp, None), P(None, fsdp)),
        out_specs=(P(dp, fsdp), P(dp, fsdp), P(both, None), P(fsdp, None), P(None, fsdp)),
        check_vma=False,
    )
```

```python
import jax
import jax.numpy as jnp
import numpy as np
from jax import lax
from jax.sharding import Mesh, PartitionSpec as P

inv_temp = 20.0
eps = 1e-06
bf16 = jnp.bfloat16
f32 = jnp.float32


def exchange(x, axes):
    return lax.all_to_all(x, axes, split_axis=0, concat_axis=0, tiled=False)


def spread(x, count):
    return jnp.broadcast_to(x[None], (count,) + x.shape)


def swap(x, axis):
    return lax.ppermute(x, axis, [(0, 1), (1, 0)])


def in_order(first, mine, other):
    return jnp.where(first, jnp.stack([mine, other]), jnp.stack([other, mine]))


def split2(v):
    high = v.astype(bf16)
    return high, (v - high.astype(f32)).astype(bf16)


def halve(v, axis, name, bit):
    mine = lax.axis_index(name) // bit % 2 == 0
    low, high = lax.index_in_dim(v, 0, axis, False), lax.index_in_dim(v, 1, axis, False)
    got = lax.ppermute(jnp.where(mine, high, low), name, [(i, i ^ bit) for i in range(4)])
    kept = jnp.where(mine, low, high)
    return jnp.where(mine, jnp.stack([kept, got], axis), jnp.stack([got, kept], axis))


def local(queries, passages, positive, hidden, lengths, w_down, w_up):
    zl_n, y_n, x_n = lax.axis_size("zl"), lax.axis_size("y"), lax.axis_size("x")
    c, y, h, x = (lax.axis_index(a) for a in ("c", "y", "h", "x"))
    plane = y_n * x_n
    rows, width = queries.shape
    pages, rank = lengths.shape[0], w_down.shape[1]
    tokens = hidden.shape[0]
    half = plane * pages
    cols = zl_n * half
    own = rows // plane

    down_c = lax.dynamic_slice_in_dim(w_down, c * (width // 2), width // 2)
    both = jnp.concatenate([queries, down_c, w_up], axis=0)
    both = in_order(h == 0, both, swap(both, "h"))
    q_mine, w_both = both[:, :rows], both[:, rows : rows + width // 2]
    up2 = both[:, rows + width // 2 :]
    q_both = in_order(c == 0, q_mine, swap(q_mine, "c"))
    q_all = q_both.transpose(0, 2, 1, 3).reshape(2 * rows, 2 * width)

    p_sub = passages.reshape(y_n, 2, x_n * pages, width).transpose(1, 0, 2, 3)
    p_sub = p_sub.reshape(2, half, width)
    p_got = exchange(spread(p_sub, zl_n).reshape(zl_n * 2, half, width), ("zl", "h"))
    p_all = p_got.reshape(zl_n, 2, half, width).transpose(0, 2, 1, 3)
    p_all = p_all.reshape(cols, 2 * width)

    part = lax.dot_general(q_all, p_all, (((1,), (1,)), ((), ())), preferred_element_type=f32)
    q_own = jnp.where(c == 0, jnp.stack([queries, q_both[1, h]]), jnp.stack([q_both[0, h], queries]))
    q_own = q_own.reshape(2 * rows, width)
    side = lax.broadcasted_iota(jnp.int32, (1, width), 1) // (width // 2) == c
    q_side = jnp.where(side, q_own, jnp.zeros_like(q_own))
    qw_part = lax.dot_general(q_side, w_up, (((1,), (1,)), ((), ())), preferred_element_type=f32)
    sent = jnp.concatenate([part, qw_part], axis=1).reshape(2 * plane, own, cols + rank)
    got = exchange(sent, ("c", "y", "x"))
    xf = hidden.astype(f32)
    rs = lax.rsqrt(jnp.mean(xf * xf, axis=-1, keepdims=True) + eps)
    got, w_both, rs = lax.optimization_barrier((got, w_both, rs))
    got = jnp.sum(got.reshape(2, plane, own, cols + rank), axis=1)
    scores = inv_temp * got[:, :, :cols]
    qw = got[0, :, cols:] + got[1, :, cols:]
    top = jnp.max(scores, axis=(0, 2))
    e = jnp.exp(scores - top[None, :, None])
    total = jnp.sum(e, axis=(0, 2))
    lane = lax.broadcasted_iota(jnp.int32, (own, rank), 1)
    stats = jnp.where(lane < rank // 2, top[:, None], total[:, None])
    stats = swap(jnp.concatenate([stats, qw], axis=0), "h")
    w_half = exchange(spread(w_both, plane), ("y", "x"))
    top_o, total_o = stats[:own, 0], stats[:own, rank // 2]
    qw = qw + stats[own:]
    top_a = jnp.maximum(top, top_o)
    scale = jnp.exp(top - top_a)
    z = total * scale + total_o * jnp.exp(top_o - top_a)
    probs = e * (scale / z)[None, :, None]
    k = np.arange(cols)
    base = k // half * (4 * half) + k % half // (x_n * pages) * (2 * x_n * pages) + k % (x_n * pages)
    base = np.stack([base, base + 2 * half]).astype(np.int32)
    target = lax.dynamic_slice(positive, ((y * x_n + x) * own,), (own,)) - h * (x_n * pages)
    onehot = (target[None, :, None] == base[:, None, :]).astype(f32)
    coeff_own = (probs - onehot).astype(bf16)

    sent = jnp.broadcast_to(qw.astype(bf16)[None], (2, own, rank))
    sent = jnp.concatenate([coeff_own, sent], axis=2)
    step = cols + rank
    sent = jnp.broadcast_to(sent[:, None], (2, plane, own, step))
    sent, w_half = lax.optimization_barrier((sent, w_half))
    got = exchange(sent.reshape(2 * plane, own, step), ("c", "y", "x"))

    wd = in_order(c == 0, w_half, swap(w_half, "c")).reshape(2, y_n, x_n, 2, width // 2, rank)
    wd = wd.transpose(1, 3, 2, 0, 4, 5).reshape(-1, rank)
    normed = (xf * rs).astype(bf16)
    pre = jnp.dot(normed, wd, preferred_element_type=f32)
    sig = jax.nn.sigmoid(pre)
    act = (pre * sig).astype(bf16)
    span = tokens // pages
    place = jnp.arange(tokens, dtype=jnp.int32)
    page_of, at = place // span, place % span
    mask = (page_of[None, :] == jnp.arange(pages)[:, None]) & (at[None, :] < lengths[:, None])
    mask = mask.astype(bf16)
    inv_len = 1.0 / lengths.astype(f32)
    x_mean = jnp.dot(mask, hidden, preferred_element_type=f32) * inv_len[:, None]
    pooled = (jnp.dot(mask, act, preferred_element_type=f32) * inv_len[:, None]).astype(bf16)
    weight = (at.reshape(pages, span) < lengths[:, None]).astype(f32) * inv_len[:, None]
    g = (sig * (1.0 + pre * (1.0 - sig)) * rs).reshape(pages, span, rank) * weight[:, :, None]

    got, pooled, g = lax.optimization_barrier((got, pooled, g))
    got = got.reshape(2 * rows, step)
    coeff, qw_all = got[:, :cols], got[:, cols:]

    c_mine = coeff.reshape(2 * rows, zl_n, plane, pages)
    c_mine = lax.dynamic_slice_in_dim(c_mine, y * x_n + x, 1, axis=2)[:, :, 0]
    dact_part = lax.dot_general(
        c_mine.reshape(2 * rows, zl_n * pages), qw_all, (((0,), (0,)), ((), ())), preferred_element_type=f32
    )
    high, low = split2(dact_part.reshape(zl_n, pages, rank))
    gq = jnp.dot(coeff, p_all, preferred_element_type=f32).reshape(2, rows, 2 * width)
    got = exchange(jnp.concatenate([high, low, spread(pooled, zl_n)], axis=1), ("zl",))
    got, x_mean = lax.optimization_barrier((got, x_mean))
    dact = inv_temp * jnp.sum(got[:, : 2 * pages].astype(f32).reshape(zl_n, 2, pages, rank), axis=(0, 1))
    pooled_zl = got[:, 2 * pages :].reshape(zl_n * pages, rank)

    dpre = (g * dact[:, None, :]).astype(bf16).reshape(tokens, rank)
    down = lax.dot_general(dpre, hidden, (((0,), (0,)), ((), ())), preferred_element_type=f32)
    first, second = jnp.split(down.astype(bf16), 2)
    theirs = swap(jnp.where(c == 0, second, first), "c")
    down = (jnp.where(c == 0, first, second).astype(f32) + theirs.astype(f32)).astype(bf16)
    down = down.reshape(rank // 2, y_n, 2, x_n, width).transpose(1, 3, 2, 0, 4).reshape(plane, rank, width)
    sent = jnp.concatenate([down, spread(pooled_zl, plane)], axis=1)
    sent, gq = lax.optimization_barrier((sent, gq))
    got = exchange(sent, ("y", "x"))
    gq_0, gq_1 = gq[:, :, :width], gq[:, :, width:]
    gq = jnp.where(h == 0, gq_0, gq_1) + swap(jnp.where(h == 0, gq_1, gq_0).astype(bf16), "h").astype(f32)
    pooled_all = got[:, rank:].reshape(plane, zl_n, pages, rank).transpose(1, 0, 2, 3).reshape(cols, rank)
    down = jnp.sum(got[:, :rank].astype(f32), axis=0).astype(bf16)
    down = down.reshape(2, zl_n, rank // 2 // zl_n, width).transpose(1, 0, 2, 3)

    lift = lax.dynamic_index_in_dim(pooled_all.reshape(zl_n, half, rank), lax.axis_index("zl"), 0, False)
    lift = jnp.einsum("pr,hrf->phf", lift, up2, preferred_element_type=f32)
    lift = lift.reshape(2, 2, 2, 2, pages, 2 * width)

    gp = lax.dot_general(coeff, q_all, (((0,), (0,)), ((), ())), preferred_element_type=f32)
    gp = gp.astype(bf16).reshape(zl_n, half, 2, width).transpose(0, 2, 1, 3)
    u = (inv_temp * jnp.dot(coeff, pooled_all, preferred_element_type=f32)).astype(bf16)
    up_part = lax.dot_general(u, q_all, (((0,), (0,)), ((), ())), preferred_element_type=f32)
    up_part = up_part.astype(bf16).reshape(zl_n, rank // zl_n, 2, width).transpose(0, 2, 1, 3)
    sent = jnp.concatenate([down, up_part, gp], axis=2)
    sent, gq, lift = lax.optimization_barrier((sent, gq, lift))
    got = exchange(sent.reshape(zl_n * 2, -1, width), ("zl", "h"))
    lift = halve(halve(halve(lift, 2, "x", 2), 3, "x", 1), 0, "y", 2)
    gq = jnp.where(c == 0, gq[0], gq[1]) + swap(jnp.where(c == 0, gq[1], gq[0]), "c")
    grad_queries = (inv_temp * gq).astype(bf16)
    got, lift = lax.optimization_barrier((got, lift))
    got = got.astype(f32)
    lift = halve(lift, 1, "y", 1).reshape(y_n, x_n, pages, 2, width)
    sub_embed = (x_mean + lift.transpose(2, 0, 3, 1, 4).reshape(pages, -1)).astype(bf16)
    n = rank // 2 // zl_n
    step = n + rank // zl_n
    weights = jnp.sum(got[:, :step], axis=0)
    gp = jnp.sum(got[:, step:].reshape(zl_n, 2, half, width), axis=0) * inv_temp
    grad_passages = gp.reshape(2, y_n, x_n * pages, width).transpose(1, 0, 2, 3)
    grad_passages = grad_passages.reshape(-1, width).astype(bf16)
    got = exchange(spread(weights, zl_n * 2), ("zl", "c")).reshape(zl_n, 2, step, width)
    grad_down = got[:, :, :n].transpose(1, 0, 2, 3).reshape(rank, width).T
    grad_up = jnp.sum(got[:, :, n:], axis=1).reshape(rank, width)
    return (grad_queries, grad_passages, sub_embed, grad_down, grad_up)


def solution(mesh):
    dp, fsdp = ("zl", "c"), ("y", "h", "x")
    shape = (mesh.shape["dp"] // 2, 2, 4, 2, mesh.shape["fsdp"] // 8)
    inner = Mesh(mesh.devices.reshape(shape), dp + fsdp)
    both = dp + fsdp
    return jax.shard_map(
        local,
        mesh=inner,
        in_specs=(P(dp, fsdp), P(dp, fsdp), P(dp), P(both, None), P(both), P(fsdp, None), P(None, fsdp)),
        out_specs=(P(dp, fsdp), P(dp, fsdp), P(both, None), P(fsdp, None), P(None, fsdp)),
        check_vma=False,
    )
```

```python
import jax
import jax.numpy as jnp
import numpy as np
from jax import lax
from jax.sharding import Mesh, PartitionSpec as P

inv_temp = 20.0
eps = 1e-06
bf16 = jnp.bfloat16
f32 = jnp.float32


def exchange(x, axes):
    return lax.all_to_all(x, axes, split_axis=0, concat_axis=0, tiled=False)


def spread(x, count):
    return jnp.broadcast_to(x[None], (count,) + x.shape)


def swap(x, axis):
    return lax.ppermute(x, axis, [(0, 1), (1, 0)])


def in_order(first, mine, other):
    return jnp.where(first, jnp.stack([mine, other]), jnp.stack([other, mine]))


def split2(v):
    high = v.astype(bf16)
    return high, (v - high.astype(f32)).astype(bf16)


def halve(v, axis, name, bit):
    mine = lax.axis_index(name) // bit % 2 == 0
    low, high = lax.index_in_dim(v, 0, axis, False), lax.index_in_dim(v, 1, axis, False)
    got = lax.ppermute(jnp.where(mine, high, low), name, [(i, i ^ bit) for i in range(4)])
    kept = jnp.where(mine, low, high)
    return jnp.where(mine, jnp.stack([kept, got], axis), jnp.stack([got, kept], axis))


def local(queries, passages, positive, hidden, lengths, w_down, w_up):
    zl_n, y_n, x_n = lax.axis_size("zl"), lax.axis_size("y"), lax.axis_size("x")
    c, y, h, x = (lax.axis_index(a) for a in ("c", "y", "h", "x"))
    plane = y_n * x_n
    rows, width = queries.shape
    pages, rank = lengths.shape[0], w_down.shape[1]
    tokens = hidden.shape[0]
    half = plane * pages
    cols = zl_n * half
    own = rows // plane

    down_c = lax.dynamic_slice_in_dim(w_down, c * (width // 2), width // 2)
    both = jnp.concatenate([queries, down_c, w_up], axis=0)
    both = in_order(h == 0, both, swap(both, "h"))
    q_mine, w_both = both[:, :rows], both[:, rows : rows + width // 2]
    up2 = both[:, rows + width // 2 :]
    q_both = in_order(c == 0, q_mine, swap(q_mine, "c"))
    q_all = q_both.transpose(0, 2, 1, 3).reshape(2 * rows, 2 * width)

    p_sub = passages.reshape(y_n, 2, x_n * pages, width).transpose(1, 0, 2, 3)
    p_sub = p_sub.reshape(2, half, width)
    p_got = exchange(spread(p_sub, zl_n).reshape(zl_n * 2, half, width), ("zl", "h"))
    p_all = p_got.reshape(zl_n, 2, half, width).transpose(0, 2, 1, 3)
    p_all = p_all.reshape(cols, 2 * width)

    part = lax.dot_general(q_all, p_all, (((1,), (1,)), ((), ())), preferred_element_type=f32)
    sent = part.reshape(2 * plane, own, cols)
    got = exchange(sent, ("c", "y", "x"))
    xf = hidden.astype(f32)
    rs = lax.rsqrt(jnp.mean(xf * xf, axis=-1, keepdims=True) + eps)
    got, w_both, rs = lax.optimization_barrier((got, w_both, rs))
    scores = inv_temp * jnp.sum(got.reshape(2, plane, own, cols), axis=1)
    top = jnp.max(scores, axis=(0, 2))
    e = jnp.exp(scores - top[None, :, None])
    total = jnp.sum(e, axis=(0, 2))
    lane = lax.broadcasted_iota(jnp.int32, (own, rank), 1)
    stats = jnp.where(lane < rank // 2, top[:, None], total[:, None])
    stats = swap(stats, "h")

    up_c = jnp.where(c == 0, up2[:, : rank // 2], up2[:, rank // 2 :]).transpose(1, 0, 2).reshape(rank // 2, -1)
    qw = lax.dot_general(q_all, up_c, (((1,), (1,)), ((), ())), preferred_element_type=f32)
    qw = qw.reshape(2, plane, own, rank // 2).transpose(1, 2, 0, 3).reshape(plane, own, rank)
    high, low = split2(qw)
    sent = jnp.concatenate([spread(w_both.reshape(width, rank), plane), high, low], axis=1)
    w_half = exchange(sent, ("y", "x"))
    top_o, total_o = stats[:own, 0], stats[:own, rank // 2]
    top_a = jnp.maximum(top, top_o)
    scale = jnp.exp(top - top_a)
    z = total * scale + total_o * jnp.exp(top_o - top_a)
    probs = e * (scale / z)[None, :, None]
    k = np.arange(cols)
    base = k // half * (4 * half) + k % half // (x_n * pages) * (2 * x_n * pages) + k % (x_n * pages)
    base = np.stack([base, base + 2 * half]).astype(np.int32)
    target = lax.dynamic_slice(positive, ((y * x_n + x) * own,), (own,)) - h * (x_n * pages)
    onehot = (target[None, :, None] == base[:, None, :]).astype(f32)
    coeff_own = (probs - onehot).astype(bf16)

    qw = jnp.sum(w_half[:, width:].astype(f32).reshape(plane, 2, own, rank), axis=(0, 1))
    w_half = w_half[:, :width]
    sent = jnp.broadcast_to(qw.astype(bf16)[None], (2, own, rank))
    sent = jnp.concatenate([coeff_own, sent], axis=2)
    step = cols + rank
    sent = jnp.broadcast_to(sent[:, None], (2, plane, own, step))
    sent, w_half = lax.optimization_barrier((sent, w_half))
    got = exchange(sent.reshape(2 * plane, own, step), ("c", "y", "x"))

    wd = in_order(c == 0, w_half, swap(w_half, "c")).reshape(2, y_n, x_n, 2, width // 2, rank)
    wd = wd.transpose(1, 3, 2, 0, 4, 5).reshape(-1, rank)
    normed = (xf * rs).astype(bf16)
    pre = jnp.dot(normed, wd, preferred_element_type=f32)
    sig = jax.nn.sigmoid(pre)
    act = (pre * sig).astype(bf16)
    span = tokens // pages
    place = jnp.arange(tokens, dtype=jnp.int32)
    page_of, at = place // span, place % span
    mask = (page_of[None, :] == jnp.arange(pages)[:, None]) & (at[None, :] < lengths[:, None])
    mask = mask.astype(bf16)
    inv_len = 1.0 / lengths.astype(f32)
    x_mean = jnp.dot(mask, hidden, preferred_element_type=f32) * inv_len[:, None]
    pooled = (jnp.dot(mask, act, preferred_element_type=f32) * inv_len[:, None]).astype(bf16)
    weight = (at.reshape(pages, span) < lengths[:, None]).astype(f32) * inv_len[:, None]
    g = (sig * (1.0 + pre * (1.0 - sig)) * rs).reshape(pages, span, rank) * weight[:, :, None]

    got, pooled, g = lax.optimization_barrier((got, pooled, g))
    got = got.reshape(2 * rows, step)
    coeff = got[:, :cols]
    qw_all = got[:, cols:].reshape(2, plane, own, 2, rank // 2).transpose(3, 1, 2, 0, 4).reshape(2 * rows, rank)

    c_mine = coeff.reshape(2 * rows, zl_n, plane, pages)
    c_mine = lax.dynamic_slice_in_dim(c_mine, y * x_n + x, 1, axis=2)[:, :, 0]
    dact_part = lax.dot_general(
        c_mine.reshape(2 * rows, zl_n * pages), qw_all, (((0,), (0,)), ((), ())), preferred_element_type=f32
    )
    high, low = split2(dact_part.reshape(zl_n, pages, rank))
    gq = jnp.dot(coeff, p_all, preferred_element_type=f32).reshape(2, rows, 2 * width)
    got = exchange(jnp.concatenate([high, low, spread(pooled, zl_n)], axis=1), ("zl",))
    got, x_mean = lax.optimization_barrier((got, x_mean))
    dact = inv_temp * jnp.sum(got[:, : 2 * pages].astype(f32).reshape(zl_n, 2, pages, rank), axis=(0, 1))
    pooled_zl = got[:, 2 * pages :].reshape(zl_n * pages, rank)

    dpre = (g * dact[:, None, :]).astype(bf16).reshape(tokens, rank)
    down = lax.dot_general(dpre, hidden, (((0,), (0,)), ((), ())), preferred_element_type=f32)
    first, second = jnp.split(down.astype(bf16), 2)
    theirs = swap(jnp.where(c == 0, second, first), "c")
    down = (jnp.where(c == 0, first, second).astype(f32) + theirs.astype(f32)).astype(bf16)
    down = down.reshape(rank // 2, y_n, 2, x_n, width).transpose(1, 3, 2, 0, 4).reshape(plane, rank, width)
    sent = jnp.concatenate([down, spread(pooled_zl, plane)], axis=1)
    sent, gq = lax.optimization_barrier((sent, gq))
    got = exchange(sent, ("y", "x"))
    gq_0, gq_1 = gq[:, :, :width], gq[:, :, width:]
    gq = jnp.where(h == 0, gq_0, gq_1) + swap(jnp.where(h == 0, gq_1, gq_0).astype(bf16), "h").astype(f32)
    pooled_all = got[:, rank:].reshape(plane, zl_n, pages, rank).transpose(1, 0, 2, 3).reshape(cols, rank)
    down = jnp.sum(got[:, :rank].astype(f32), axis=0).astype(bf16)
    down = down.reshape(2, zl_n, rank // 2 // zl_n, width).transpose(1, 0, 2, 3)

    lift = lax.dynamic_index_in_dim(pooled_all.reshape(zl_n, half, rank), lax.axis_index("zl"), 0, False)
    lift = jnp.einsum("pr,hrf->phf", lift, up2, preferred_element_type=f32)
    lift = lift.reshape(2, 2, 2, 2, pages, 2 * width)

    gp = lax.dot_general(coeff, q_all, (((0,), (0,)), ((), ())), preferred_element_type=f32)
    gp = gp.astype(bf16).reshape(zl_n, half, 2, width).transpose(0, 2, 1, 3)
    u = (inv_temp * jnp.dot(coeff, pooled_all, preferred_element_type=f32)).astype(bf16)
    up_part = lax.dot_general(u, q_all, (((0,), (0,)), ((), ())), preferred_element_type=f32)
    up_part = up_part.astype(bf16).reshape(zl_n, rank // zl_n, 2, width).transpose(0, 2, 1, 3)
    sent = jnp.concatenate([down, up_part, gp], axis=2)
    sent, gq = lax.optimization_barrier((sent, gq))
    got = exchange(sent.reshape(zl_n * 2, -1, width), ("zl", "h"))
    gq = jnp.where(c == 0, gq[0], gq[1]) + swap(jnp.where(c == 0, gq[1], gq[0]), "c")
    gq, lift = lax.optimization_barrier((gq, lift))
    lift = halve(halve(halve(lift, 2, "x", 2), 3, "x", 1), 0, "y", 2)
    grad_queries = (inv_temp * gq).astype(bf16)
    got, lift = lax.optimization_barrier((got, lift))
    got = got.astype(f32)
    lift = halve(lift, 1, "y", 1).reshape(y_n, x_n, pages, 2, width)
    sub_embed = (x_mean + lift.transpose(2, 0, 3, 1, 4).reshape(pages, -1)).astype(bf16)
    n = rank // 2 // zl_n
    step = n + rank // zl_n
    weights = jnp.sum(got[:, :step], axis=0)
    gp = jnp.sum(got[:, step:].reshape(zl_n, 2, half, width), axis=0) * inv_temp
    grad_passages = gp.reshape(2, y_n, x_n * pages, width).transpose(1, 0, 2, 3)
    grad_passages = grad_passages.reshape(-1, width).astype(bf16)
    got = exchange(spread(weights, zl_n * 2), ("zl", "c")).reshape(zl_n, 2, step, width)
    grad_down = got[:, :, :n].transpose(1, 0, 2, 3).reshape(rank, width).T
    grad_up = jnp.sum(got[:, :, n:], axis=1).reshape(rank, width)
    return (grad_queries, grad_passages, sub_embed, grad_down, grad_up)


def solution(mesh):
    dp, fsdp = ("zl", "c"), ("y", "h", "x")
    shape = (mesh.shape["dp"] // 2, 2, 4, 2, mesh.shape["fsdp"] // 8)
    inner = Mesh(mesh.devices.reshape(shape), dp + fsdp)
    both = dp + fsdp
    return jax.shard_map(
        local,
        mesh=inner,
        in_specs=(P(dp, fsdp), P(dp, fsdp), P(dp), P(both, None), P(both), P(fsdp, None), P(None, fsdp)),
        out_specs=(P(dp, fsdp), P(dp, fsdp), P(both, None), P(fsdp, None), P(None, fsdp)),
        check_vma=False,
    )
```

```python
import jax
import jax.numpy as jnp
import numpy as np
from jax import lax
from jax.sharding import Mesh, PartitionSpec as P

inv_temp = 20.0
eps = 1e-06
bf16 = jnp.bfloat16
f32 = jnp.float32


def exchange(x, axes):
    return lax.all_to_all(x, axes, split_axis=0, concat_axis=0, tiled=False)


def spread(x, count):
    return jnp.broadcast_to(x[None], (count,) + x.shape)


def swap(x, axis):
    return lax.ppermute(x, axis, [(0, 1), (1, 0)])


def in_order(first, mine, other):
    return jnp.where(first, jnp.stack([mine, other]), jnp.stack([other, mine]))


def split2(v):
    high = v.astype(bf16)
    return high, (v - high.astype(f32)).astype(bf16)


def halve(v, axis, name, bit):
    mine = lax.axis_index(name) // bit % 2 == 0
    low, high = lax.index_in_dim(v, 0, axis, False), lax.index_in_dim(v, 1, axis, False)
    got = lax.ppermute(jnp.where(mine, high, low), name, [(i, i ^ bit) for i in range(4)])
    kept = jnp.where(mine, low, high)
    return jnp.where(mine, jnp.stack([kept, got], axis), jnp.stack([got, kept], axis))


def local(queries, passages, positive, hidden, lengths, w_down, w_up):
    zl_n, y_n, x_n = lax.axis_size("zl"), lax.axis_size("y"), lax.axis_size("x")
    c, y, h, x = (lax.axis_index(a) for a in ("c", "y", "h", "x"))
    plane = y_n * x_n
    rows, width = queries.shape
    pages, rank = lengths.shape[0], w_down.shape[1]
    tokens = hidden.shape[0]
    half = plane * pages
    cols = zl_n * half
    own = rows // plane

    down_c = lax.dynamic_slice_in_dim(w_down, c * (width // 2), width // 2)
    both = jnp.concatenate([queries, down_c, w_up], axis=0)
    both = in_order(h == 0, both, swap(both, "h"))
    q_mine, w_both = both[:, :rows], both[:, rows : rows + width // 2]
    up2 = both[:, rows + width // 2 :]
    q_both = in_order(c == 0, q_mine, swap(q_mine, "c"))
    q_all = q_both.transpose(0, 2, 1, 3).reshape(2 * rows, 2 * width)

    p_sub = passages.reshape(y_n, 2, x_n * pages, width).transpose(1, 0, 2, 3)
    p_sub = p_sub.reshape(2, half, width)
    p_got = exchange(spread(p_sub, zl_n).reshape(zl_n * 2, half, width), ("zl", "h"))
    p_all = p_got.reshape(zl_n, 2, half, width).transpose(0, 2, 1, 3)
    p_all = p_all.reshape(cols, 2 * width)

    part = lax.dot_general(q_all, p_all, (((1,), (1,)), ((), ())), preferred_element_type=f32)
    sent = part.reshape(2 * plane, own, cols)
    got = exchange(sent, ("c", "y", "x"))
    xf = hidden.astype(f32)
    rs = lax.rsqrt(jnp.mean(xf * xf, axis=-1, keepdims=True) + eps)
    got, w_both, rs = lax.optimization_barrier((got, w_both, rs))
    scores = inv_temp * jnp.sum(got.reshape(2, plane, own, cols), axis=1)
    top = jnp.max(scores, axis=(0, 2))
    e = jnp.exp(scores - top[None, :, None])
    total = jnp.sum(e, axis=(0, 2))
    lane = lax.broadcasted_iota(jnp.int32, (own, rank), 1)
    stats = jnp.where(lane < rank // 2, top[:, None], total[:, None])
    stats = swap(stats, "h")

    up_c = jnp.where(c == 0, up2[:, : rank // 2], up2[:, rank // 2 :]).transpose(1, 0, 2).reshape(rank // 2, -1)
    qw = lax.dot_general(q_all, up_c, (((1,), (1,)), ((), ())), preferred_element_type=f32)
    qw = qw.reshape(2, plane, own, rank // 2).transpose(1, 2, 0, 3).reshape(plane, own, rank)
    high, low = split2(qw)
    sent = jnp.concatenate([spread(w_both.reshape(width, rank), plane), high, low], axis=1)
    w_half = exchange(sent, ("y", "x"))
    top_o, total_o = stats[:own, 0], stats[:own, rank // 2]
    top_a = jnp.maximum(top, top_o)
    scale = jnp.exp(top - top_a)
    z = total * scale + total_o * jnp.exp(top_o - top_a)
    probs = e * (scale / z)[None, :, None]
    k = np.arange(cols)
    base = k // half * (4 * half) + k % half // (x_n * pages) * (2 * x_n * pages) + k % (x_n * pages)
    base = np.stack([base, base + 2 * half]).astype(np.int32)
    target = lax.dynamic_slice(positive, ((y * x_n + x) * own,), (own,)) - h * (x_n * pages)
    onehot = (target[None, :, None] == base[:, None, :]).astype(f32)
    coeff_own = (probs - onehot).astype(bf16)

    qw = jnp.sum(w_half[:, width:].astype(f32).reshape(plane, 2, own, rank), axis=(0, 1))
    w_half = w_half[:, :width]
    sent = jnp.broadcast_to(qw.astype(bf16)[None], (2, own, rank))
    sent = jnp.concatenate([coeff_own, sent], axis=2)
    step = cols + rank
    sent = jnp.broadcast_to(sent[:, None], (2, plane, own, step))
    sent, w_half = lax.optimization_barrier((sent, w_half))
    got = exchange(sent.reshape(2 * plane, own, step), ("c", "y", "x"))

    wd = in_order(c == 0, w_half, swap(w_half, "c")).reshape(2, y_n, x_n, 2, width // 2, rank)
    wd = wd.transpose(1, 3, 2, 0, 4, 5).reshape(-1, rank)
    normed = (xf * rs).astype(bf16)
    pre = jnp.dot(normed, wd, preferred_element_type=f32)
    sig = jax.nn.sigmoid(pre)
    act = (pre * sig).astype(bf16)
    span = tokens // pages
    place = jnp.arange(tokens, dtype=jnp.int32)
    page_of, at = place // span, place % span
    mask = (page_of[None, :] == jnp.arange(pages)[:, None]) & (at[None, :] < lengths[:, None])
    mask = mask.astype(bf16)
    inv_len = 1.0 / lengths.astype(f32)
    x_mean = jnp.dot(mask, hidden, preferred_element_type=f32) * inv_len[:, None]
    pooled = (jnp.dot(mask, act, preferred_element_type=f32) * inv_len[:, None]).astype(bf16)
    weight = (at.reshape(pages, span) < lengths[:, None]).astype(f32) * inv_len[:, None]
    g = (sig * (1.0 + pre * (1.0 - sig)) * rs).reshape(pages, span, rank) * weight[:, :, None]

    got, pooled, g = lax.optimization_barrier((got, pooled, g))
    got = got.reshape(2 * rows, step)
    coeff = got[:, :cols]
    qw_all = got[:, cols:].reshape(2, plane, own, 2, rank // 2).transpose(3, 1, 2, 0, 4).reshape(2 * rows, rank)

    c_mine = coeff.reshape(2 * rows, zl_n, plane, pages)
    c_mine = lax.dynamic_slice_in_dim(c_mine, y * x_n + x, 1, axis=2)[:, :, 0]
    dact_part = lax.dot_general(
        c_mine.reshape(2 * rows, zl_n * pages), qw_all, (((0,), (0,)), ((), ())), preferred_element_type=f32
    )
    high, low = split2(dact_part.reshape(zl_n, pages, rank))
    gq = jnp.dot(coeff, p_all, preferred_element_type=f32).reshape(2, rows, 2 * width)
    got = exchange(jnp.concatenate([high, low, spread(pooled, zl_n)], axis=1), ("zl",))
    got, x_mean = lax.optimization_barrier((got, x_mean))
    dact = inv_temp * jnp.sum(got[:, : 2 * pages].astype(f32).reshape(zl_n, 2, pages, rank), axis=(0, 1))
    pooled_zl = got[:, 2 * pages :].reshape(zl_n * pages, rank)

    dpre = (g * dact[:, None, :]).astype(bf16).reshape(tokens, rank)
    down = lax.dot_general(dpre, hidden, (((0,), (0,)), ((), ())), preferred_element_type=f32)
    first, second = jnp.split(down.astype(bf16), 2)
    theirs = swap(jnp.where(c == 0, second, first), "c")
    down = (jnp.where(c == 0, first, second).astype(f32) + theirs.astype(f32)).astype(bf16)
    down = down.reshape(rank // 2, y_n, 2, x_n, width).transpose(1, 3, 2, 0, 4).reshape(plane, rank, width)
    sent = jnp.concatenate([down, spread(pooled_zl, plane)], axis=1)
    sent, gq = lax.optimization_barrier((sent, gq))
    got = exchange(sent, ("y", "x"))
    gq_0, gq_1 = gq[:, :, :width], gq[:, :, width:]
    gq = jnp.where(h == 0, gq_0, gq_1) + swap(jnp.where(h == 0, gq_1, gq_0).astype(bf16), "h").astype(f32)
    pooled_all = got[:, rank:].reshape(plane, zl_n, pages, rank).transpose(1, 0, 2, 3).reshape(cols, rank)
    down = jnp.sum(got[:, :rank].astype(f32), axis=0).astype(bf16)
    down = down.reshape(2, zl_n, rank // 2 // zl_n, width).transpose(1, 0, 2, 3)

    lift = lax.dynamic_index_in_dim(pooled_all.reshape(zl_n, half, rank), lax.axis_index("zl"), 0, False)
    lift = jnp.einsum("pr,hrf->phf", lift, up2, preferred_element_type=f32)
    lift = lift.reshape(2, 2, 2, 2, pages, 2 * width)

    gp = lax.dot_general(coeff, q_all, (((0,), (0,)), ((), ())), preferred_element_type=f32)
    gp = gp.astype(bf16).reshape(zl_n, half, 2, width).transpose(0, 2, 1, 3)
    u = (inv_temp * jnp.dot(coeff, pooled_all, preferred_element_type=f32)).astype(bf16)
    up_part = lax.dot_general(u, q_all, (((0,), (0,)), ((), ())), preferred_element_type=f32)
    up_part = up_part.astype(bf16).reshape(zl_n, rank // zl_n, 2, width).transpose(0, 2, 1, 3)
    sent = jnp.concatenate([down, up_part, gp], axis=2)
    got = exchange(sent.reshape(zl_n * 2, -1, width), ("zl", "h"))
    gq = jnp.where(c == 0, gq[0], gq[1]) + swap(jnp.where(c == 0, gq[1], gq[0]), "c")
    gq, lift = lax.optimization_barrier((gq, lift))
    lift = halve(halve(halve(lift, 2, "x", 2), 3, "x", 1), 0, "y", 2)
    grad_queries = (inv_temp * gq).astype(bf16)
    got, lift = lax.optimization_barrier((got, lift))
    got = got.astype(f32)
    lift = halve(lift, 1, "y", 1).reshape(y_n, x_n, pages, 2, width)
    sub_embed = (x_mean + lift.transpose(2, 0, 3, 1, 4).reshape(pages, -1)).astype(bf16)
    n = rank // 2 // zl_n
    step = n + rank // zl_n
    weights = jnp.sum(got[:, :step], axis=0)
    gp = jnp.sum(got[:, step:].reshape(zl_n, 2, half, width), axis=0) * inv_temp
    grad_passages = gp.reshape(2, y_n, x_n * pages, width).transpose(1, 0, 2, 3)
    grad_passages = grad_passages.reshape(-1, width).astype(bf16)
    got = exchange(spread(weights, zl_n * 2), ("zl", "c")).reshape(zl_n, 2, step, width)
    grad_down = got[:, :, :n].transpose(1, 0, 2, 3).reshape(rank, width).T
    grad_up = jnp.sum(got[:, :, n:], axis=1).reshape(rank, width)
    return (grad_queries, grad_passages, sub_embed, grad_down, grad_up)


def solution(mesh):
    dp, fsdp = ("zl", "c"), ("y", "h", "x")
    shape = (mesh.shape["dp"] // 2, 2, 4, 2, mesh.shape["fsdp"] // 8)
    inner = Mesh(mesh.devices.reshape(shape), dp + fsdp)
    both = dp + fsdp
    return jax.shard_map(
        local,
        mesh=inner,
        in_specs=(P(dp, fsdp), P(dp, fsdp), P(dp), P(both, None), P(both), P(fsdp, None), P(None, fsdp)),
        out_specs=(P(dp, fsdp), P(dp, fsdp), P(both, None), P(fsdp, None), P(None, fsdp)),
        check_vma=False,
    )
```
